32 devices in a mesh: dp: 8 (over z, y), table: 2 (over x), rep: 2 (over core).
Axes of the slice: x: 2, y: 2, z: 4, core: 2. Of those that a mesh axis runs over, the one named last changes fastest.
Arguments:
- item_table: bfloat16 [3072, 256], P('table'), may hold values from -6 to 6
- fetch_rows: int32 [32, 192], P(('dp', 'table', 'rep')), may hold values from 0 to 1535, as said below
- fetch_count: int32 [32, 2], P(('dp', 'table', 'rep')), may hold values from 1 to 96, as said below
- item_slot: int32 [12288], P(('dp', 'table', 'rep')), may hold values from 0 to 191, as said below
- action_id: int32 [12288], P(('dp', 'table', 'rep')), may hold values from 0 to 15
- lengths: int32 [32, 8], P(('dp', 'table', 'rep')), may hold values from 1 to 192, as said below
- action_table: bfloat16 [16, 256], replicated, may hold values from -6 to 6
- w_in: bfloat16 [256, 1024], replicated, may hold values from -0.375 to 0.375
- w_proj: bfloat16 [1024, 1024], replicated, may hold values from -0.1875 to 0.1875
- w_out: bfloat16 [256, 1024], replicated, may hold values from -0.375 to 0.375
- cotangent: bfloat16 [12288, 1024], P(('dp', 'table', 'rep')), may hold values from -6 to 6
Outputs:
- item_grad: float32 [49152, 256], P(('dp', 'table', 'rep'))
- grad_w_in: float32 [256, 1024], P('table')
- grad_proj: float32 [1024, 1024], P('table')
- grad_out: float32 [256, 1024], P('table')
- grad_action: float32 [16, 256], P(None, 'table')
The draws below stay inside these ranges and needn't reach their ends.
Inputs may be any that keep to these rules, and one draw needn't show every extreme that they name: `fetch_rows`: the 96 rows that one device may send to one requester are distinct. `fetch_count`: in every group of devices that share the dp and rep index, some requester receives 96 rows from every owner. `item_slot`: an event's slot lies within the rows its owner sends: owner times 96 plus a slot below that owner's count for this device. Each device's 8 lengths sum to at most 384; some device's sum to exactly 384.
All inputs are finite; a program needn't handle non-finite values.
Results may differ from the reference program's by a relative error of at most 0.012.
Values may be sent and summed in bfloat16 or wider, within the bound.
A program may use at most 64 MiB of HBM per device.

```python
import jax
import jax.numpy as jnp
from jax import lax

D = 1024
E = 256
HEADS = 2
HEAD = 128
ACTIONS = 16
SEQ_DEV = 8
TOK_DEV = 384
LMAX = 192
SLOTS = 96
FETCHED = 192
ITEMS_DEV = 1536
ITEMS = 3072
EVENTS = 12288
N_DP = 8
N_TABLE = 2
N_REP = 2
DEVICES = 32


def shared_counts(key):
    key = jax.random.fold_in(key, 101)
    first_key, second_key = jax.random.split(key)
    full = jax.random.randint(first_key, (N_DP, N_REP), 0, N_TABLE, dtype=jnp.int32)
    lowest = max(1, SLOTS // 3)
    drawn = jax.random.randint(second_key, (N_DP, N_TABLE, N_REP, N_TABLE), lowest, SLOTS + 1, dtype=jnp.int32)
    target = jnp.arange(N_TABLE, dtype=jnp.int32)[None, None, None, :] == full[:, None, :, None]
    return jnp.where(target, SLOTS, drawn).astype(jnp.int32)


def draw_fetch_rows(key, part):
    key = jax.random.fold_in(key, 7)
    blocks = DEVICES * N_TABLE
    keys = jax.random.split(key, blocks)

    def pick(one_key):
        return jax.random.permutation(one_key, ITEMS_DEV)[:SLOTS].astype(jnp.int32)
    return jax.vmap(pick)(keys).reshape(DEVICES, FETCHED)


def draw_fetch_count(key, part):
    counts = shared_counts(key)
    return counts.reshape(DEVICES, N_TABLE)


def draw_item_slot(key, part):
    counts = shared_counts(key)
    key = jax.random.fold_in(key, 11)
    per_requester = jnp.transpose(counts, (0, 3, 2, 1)).reshape(DEVICES, N_TABLE)
    keys = jax.random.split(key, DEVICES)

    def single(one_key, own_counts):
        first_key, second_key = jax.random.split(one_key)
        owner = jax.random.randint(first_key, (TOK_DEV,), 0, N_TABLE, dtype=jnp.int32)
        position = jnp.arange(TOK_DEV, dtype=jnp.int32)
        owner = jnp.where(position == 0, N_TABLE - 1, jnp.where(position == 1, 0, owner))
        limit = jnp.take(own_counts, owner)
        slot = jax.random.randint(second_key, (TOK_DEV,), 0, limit, dtype=jnp.int32)
        slot = jnp.where(position == 0, limit - 1, jnp.where(position == 1, 0, slot))
        return (owner * SLOTS + slot).astype(jnp.int32)
    return jax.vmap(single)(keys, per_requester).reshape(EVENTS)


def distribute(key, total, count):
    shares = jax.random.randint(key, (count,), 1, 5, dtype=jnp.int32)
    whole = jnp.sum(shares)
    base = 1 + (total - count) * shares // whole
    rest = total - jnp.sum(base)
    return (base + (jnp.arange(count, dtype=jnp.int32) < rest).astype(jnp.int32)).astype(jnp.int32)


def draw_lengths(key, part):
    key = jax.random.fold_in(key, 13)
    chosen_key, device_key = jax.random.split(key)
    designated = jax.random.randint(chosen_key, (), 0, DEVICES, dtype=jnp.int32)
    keys = jax.random.split(device_key, DEVICES)
    quarter = TOK_DEV // 4

    def single(one_key, device):
        load_key, split_key, other_key, place_key = jax.random.split(one_key, 4)
        level = jax.random.randint(load_key, (), 0, 8, dtype=jnp.int32)
        load = quarter + (TOK_DEV - quarter) * level * level * level // 343
        entries = distribute(split_key, load, SEQ_DEV)
        others = distribute(other_key, TOK_DEV - LMAX, SEQ_DEV - 1)
        place = jax.random.randint(place_key, (), 0, SEQ_DEV, dtype=jnp.int32)
        index = jnp.arange(SEQ_DEV, dtype=jnp.int32)
        source = jnp.clip(index - (index > place).astype(jnp.int32), 0, SEQ_DEV - 2)
        special = jnp.where(index == place, LMAX, jnp.take(others, source))
        return jnp.where(device == designated, special, entries).astype(jnp.int32)
    return jax.vmap(single)(keys, jnp.arange(DEVICES, dtype=jnp.int32))


def with_ends(array, stream_key, low, high):
    dims = array.shape
    index_at = [jax.random.randint(jax.random.fold_in(stream_key, axis), (), 0, dims[axis]) for axis in range(len(dims))]
    array = array.at[tuple(index_at)].set(low)
    longest = dims.index(max(dims))
    index_at[longest] = (index_at[longest] + 1) % dims[longest]
    return array.at[tuple(index_at)].set(high)


def shard_levels(key, dims, cuts, smallest, top_value):
    level, own = 1.0, jax.random.fold_in(key, 6)
    for dim, blocks in cuts:
        draws = jnp.exp(jax.random.uniform(jax.random.fold_in(own, dim), (blocks,), jnp.float32, smallest / len(cuts), top_value / len(cuts)))
        level = level * jnp.repeat(draws, dims[dim] // blocks).reshape([-1 if axis == dim else 1 for axis in range(len(dims))])
    return level


def bell_draw(own_key, dims, scale, bound, cuts=(), kind=jnp.bfloat16):
    factor_of = shard_levels(own_key, dims, cuts, -0.22, 0.18) if cuts else 1.0
    array = jax.random.normal(own_key, dims, jnp.float32) * scale * factor_of
    return jnp.minimum(jnp.maximum(array, -bound), bound).astype(kind)


def setup_inputs(seed: int = 0) -> dict:
    streams_of = jax.random.split(jax.random.key(seed), 12)
    return {
        "item_table": bell_draw(streams_of[0], (ITEMS, E), 1.0, 6.0, ((0, 2),)),
        "fetch_rows": draw_fetch_rows(jax.random.fold_in(streams_of[11], 71), 0),
        "fetch_count": draw_fetch_count(jax.random.fold_in(streams_of[11], 71), 0),
        "item_slot": draw_item_slot(jax.random.fold_in(streams_of[11], 71), 0),
        "action_id": with_ends(jax.random.randint(streams_of[4], (EVENTS,), 0, ACTIONS), jax.random.fold_in(streams_of[4], 1), 0, ACTIONS - 1).astype(jnp.int32),
        "lengths": draw_lengths(jax.random.fold_in(streams_of[11], 71), 0),
        "action_table": bell_draw(streams_of[6], (ACTIONS, E), 1.0, 6.0),
        "w_in": bell_draw(streams_of[7], (E, D), E ** -0.5, 0.375),
        "w_proj": bell_draw(streams_of[8], (D, 4 * HEADS * HEAD), D ** -0.5, 0.1875),
        "w_out": bell_draw(streams_of[9], (HEADS * HEAD, D), (HEADS * HEAD) ** -0.5, 0.375),
        "cotangent": bell_draw(streams_of[10], (EVENTS, D), 1.0, 6.0, ((0, 32),)),
    }


epsilon = 1e-05

def layer_norm(matrix):
    center = matrix - lax.optimization_barrier(jnp.mean(matrix, axis=-1, keepdims=True))
    spread = lax.optimization_barrier(jnp.mean(center * center, axis=-1, keepdims=True))
    return center * lax.rsqrt(spread + epsilon)

def sequence_layout(lengths, count):
    ends = jnp.cumsum(lengths, dtype=jnp.int32)
    position = jnp.arange(count, dtype=jnp.int32)
    live = position < ends[-1]
    sequence = lax.optimization_barrier(jnp.sum((position[:, None] >= ends[None, :]).astype(jnp.int32), axis=1, dtype=jnp.int32))
    chosen = sequence[:, None] == jnp.arange(lengths.shape[0], dtype=jnp.int32)[None, :]
    row_length = lax.optimization_barrier(jnp.sum(jnp.where(chosen, lengths[None, :], 0), axis=1, dtype=jnp.int32))
    allowed = (sequence[:, None] == sequence[None, :]) & (position[None, :] <= position[:, None])
    allowed = allowed & live[:, None] & live[None, :]
    safe_length = jnp.maximum(row_length, 1).astype(jnp.float32)
    inverse_length = jnp.where(live, 1.0 / safe_length, jnp.zeros_like(safe_length))
    return (allowed, inverse_length, live)

def mixing(projected, allowed, inverse_length, heads, head):
    width = heads * head
    count = projected.shape[0]
    activated = jax.nn.silu(projected)
    gating = activated[:, :width].astype(jnp.bfloat16)
    value_rows = activated[:, width:2 * width].astype(jnp.bfloat16)
    queries = activated[:, 2 * width:3 * width].astype(jnp.bfloat16)
    key_rows = activated[:, 3 * width:].astype(jnp.bfloat16)
    query_heads = queries.astype(jnp.float32).reshape(count, heads, head)
    key_heads = key_rows.astype(jnp.float32).reshape(count, heads, head)
    value_heads = value_rows.astype(jnp.float32).reshape(count, heads, head)
    scores = jnp.einsum('thd,shd->hts', query_heads, key_heads) * head ** (-0.5)
    weights = jnp.where(allowed[None], jax.nn.silu(scores), 0.0) * inverse_length[None, :, None]
    weights = weights.astype(jnp.bfloat16)
    attended = jnp.einsum('hts,shd->thd', weights.astype(jnp.float32), value_heads).reshape(count, width)
    return (layer_norm(attended) * gating.astype(jnp.float32)).astype(jnp.bfloat16)

def local_terms(fetched, item_slot, action_id, lengths, action_table, w_in, w_proj, w_out, cotangent):
    count = cotangent.shape[0]
    loss_scale = count ** (-0.5)
    allowed, inverse_length, live = sequence_layout(lengths, count)
    cotangent = jnp.where(live[:, None], cotangent, jnp.zeros_like(cotangent))
    item_rows = jnp.take(fetched, item_slot, axis=0).astype(jnp.float32)
    action_rows = jnp.take(action_table, action_id, axis=0).astype(jnp.float32)
    embedded = (item_rows + action_rows).astype(jnp.bfloat16)
    hidden = jnp.dot(embedded, w_in, preferred_element_type=jnp.float32)
    normed_full, norm_back = jax.vjp(layer_norm, hidden)
    normed = normed_full.astype(jnp.bfloat16)
    projected = jnp.dot(normed, w_proj, preferred_element_type=jnp.float32)
    mixed_rows, mix_back = jax.vjp(lambda values: mixing(values, allowed, inverse_length, HEADS, HEAD), projected)
    grad_out = jnp.dot(mixed_rows.T, cotangent, preferred_element_type=jnp.float32) * loss_scale
    grad_mixed = (jnp.dot(cotangent, w_out.T, preferred_element_type=jnp.float32) * loss_scale).astype(jnp.bfloat16)
    grad_pre = mix_back(grad_mixed)[0].astype(jnp.bfloat16)
    grad_proj = jnp.dot(normed.T, grad_pre, preferred_element_type=jnp.float32)
    grad_normed = jnp.dot(grad_pre, w_proj.T, preferred_element_type=jnp.float32)
    grad_hidden = (cotangent.astype(jnp.float32) * loss_scale + norm_back(grad_normed)[0]).astype(jnp.bfloat16)
    grad_in = jnp.dot(embedded.T, grad_hidden, preferred_element_type=jnp.float32)
    grad_embedded = jnp.dot(grad_hidden, w_in.T, preferred_element_type=jnp.float32)
    slot_grad = jax.ops.segment_sum(grad_embedded, item_slot, num_segments=fetched.shape[0])
    action_grad = jax.ops.segment_sum(grad_embedded, action_id, num_segments=action_table.shape[0])
    return ((grad_in, grad_proj, grad_out, action_grad), slot_grad)

def reference(item_table, fetch_rows, fetch_count, item_slot, action_id, lengths, action_table, w_in, w_proj, w_out, cotangent):
    requests = fetch_rows.reshape(N_DP, N_TABLE, N_REP, N_TABLE, SLOTS)
    by_requester = jnp.transpose(requests, (0, 3, 2, 1, 4))
    counts = jnp.transpose(fetch_count.reshape(N_DP, N_TABLE, N_REP, N_TABLE), (0, 3, 2, 1))
    slot_index = jnp.arange(SLOTS, dtype=jnp.int32)
    valid = (slot_index[None, None, None, None, :] < counts[:, :, :, :, None]).reshape(DEVICES, FETCHED)
    owner_index = jnp.arange(N_TABLE, dtype=jnp.int32)
    wanted = (by_requester + (owner_index * ITEMS_DEV)[None, None, None, :, None]).reshape(DEVICES, FETCHED)
    initial = (jnp.zeros((E, D), jnp.float32), jnp.zeros((D, 4 * HEADS * HEAD), jnp.float32), jnp.zeros((HEADS * HEAD, D), jnp.float32), jnp.zeros((ACTIONS, E), jnp.float32))

    def accumulate(running, inputs):
        wanted_rows, valid_rows, slot_ids, action_ids, seq_lengths, cot_rows = inputs
        taken = jnp.take(item_table, wanted_rows, axis=0)
        fetched = jnp.where(valid_rows[:, None], taken, jnp.zeros_like(taken))
        dense, slot_grad = local_terms(fetched, slot_ids, action_ids, seq_lengths, action_table, w_in, w_proj, w_out, cot_rows)
        slot_grad = jnp.where(valid_rows[:, None], slot_grad, jnp.zeros_like(slot_grad))
        return (tuple((left + right for left, right in zip(running, dense))), slot_grad)
    running, slot_grads = lax.scan(accumulate, initial, (wanted, valid, item_slot.reshape(DEVICES, TOK_DEV), action_id.reshape(DEVICES, TOK_DEV), lengths, cotangent.reshape(DEVICES, TOK_DEV, D)))
    factor = DEVICES ** (-0.5)
    data_index = jnp.arange(N_DP, dtype=jnp.int32)[:, None, None, None, None]
    rep_index = jnp.arange(N_REP, dtype=jnp.int32)[None, None, :, None, None]
    device_base = ((data_index * N_TABLE + owner_index[None, None, None, :, None]) * N_REP + rep_index) * ITEMS_DEV
    target = (device_base + by_requester).reshape(DEVICES * FETCHED)
    item_grad = jnp.zeros((DEVICES * ITEMS_DEV, E), jnp.float32).at[target].add(slot_grads.reshape(DEVICES * FETCHED, E))
    return (item_grad, running[0] * factor, running[1] * factor, running[2] * factor, running[3] * factor)
```

```python
import jax
import jax.numpy as jnp
from jax import lax
from jax.experimental import pallas as pl
from jax.experimental.pallas import tpu as pltpu
from jax.sharding import PartitionSpec as P

HEADS = 2
HEAD = 128


epsilon = 1e-05


def layer_norm(matrix):
    center = matrix - jnp.mean(matrix, axis=-1, keepdims=True)
    spread = jnp.mean(center * center, axis=-1, keepdims=True)
    return center * lax.rsqrt(spread + epsilon)


def sequence_layout(lengths, count):
    ends = jnp.cumsum(lengths, dtype=jnp.int32)
    position = jnp.arange(count, dtype=jnp.int32)
    live = position < ends[-1]
    sequence = jnp.sum(
        (position[:, None] >= ends[None, :]).astype(jnp.int32), axis=1, dtype=jnp.int32
    )
    chosen = sequence[:, None] == jnp.arange(lengths.shape[0], dtype=jnp.int32)[None, :]
    row_length = jnp.sum(jnp.where(chosen, lengths[None, :], 0), axis=1, dtype=jnp.int32)
    allowed = (sequence[:, None] == sequence[None, :]) & (position[None, :] <= position[:, None])
    allowed = allowed & live[:, None] & live[None, :]
    safe_length = jnp.maximum(row_length, 1).astype(jnp.float32)
    inverse_length = jnp.where(live, 1.0 / safe_length, jnp.zeros_like(safe_length))
    return (allowed, inverse_length, live)


def mixing(projected, allowed, inverse_length, heads, head):
    width = heads * head
    count = projected.shape[0]
    activated = jax.nn.silu(projected)
    gating = activated[:, :width].astype(jnp.bfloat16)
    value_rows = activated[:, width : 2 * width].astype(jnp.bfloat16)
    queries = activated[:, 2 * width : 3 * width].astype(jnp.bfloat16)
    key_rows = activated[:, 3 * width :].astype(jnp.bfloat16)
    query_heads = queries.reshape(count, heads, head)
    key_heads = key_rows.reshape(count, heads, head)
    value_heads = value_rows.reshape(count, heads, head)
    scores = jnp.einsum(
        "thd,shd->hts", query_heads, key_heads, preferred_element_type=jnp.float32
    ) * head ** (-0.5)
    weights = jnp.where(allowed[None], jax.nn.silu(scores), 0.0) * inverse_length[None, :, None]
    weights = weights.astype(jnp.bfloat16)
    attended = jnp.einsum(
        "hts,shd->thd", weights, value_heads, preferred_element_type=jnp.float32
    ).reshape(count, width)
    return (layer_norm(attended) * gating.astype(jnp.float32)).astype(jnp.bfloat16)


def local_terms(
    fetched, item_slot, action_id, lengths, action_table, w_in, w_proj, w_out, cotangent
):
    count = cotangent.shape[0]
    loss_scale = count ** (-0.5)
    allowed, inverse_length, live = sequence_layout(lengths, count)
    cotangent = jnp.where(live[:, None], cotangent, jnp.zeros_like(cotangent))
    item_rows = jnp.take(fetched, item_slot, axis=0)
    action_hot = action_id[:, None] == jnp.arange(action_table.shape[0], dtype=jnp.int32)[None, :]
    action_rows = jnp.dot(
        action_hot.astype(jnp.bfloat16), action_table, preferred_element_type=jnp.float32
    )
    embedded = (item_rows.astype(jnp.float32) + action_rows).astype(jnp.bfloat16)
    hidden = jnp.dot(embedded, w_in, preferred_element_type=jnp.float32)
    normed_full, norm_back = jax.vjp(layer_norm, hidden)
    normed = normed_full.astype(jnp.bfloat16)
    projected = jnp.dot(normed, w_proj, preferred_element_type=jnp.float32)
    mixed_rows, mix_back = jax.vjp(
        lambda values: mixing(values, allowed, inverse_length, HEADS, HEAD), projected
    )
    grad_out = jnp.dot(mixed_rows.T, cotangent, preferred_element_type=jnp.float32) * loss_scale
    grad_mixed = (
        jnp.dot(cotangent, w_out.T, preferred_element_type=jnp.float32) * loss_scale
    ).astype(jnp.bfloat16)
    grad_pre = mix_back(grad_mixed)[0].astype(jnp.bfloat16)
    grad_proj = jnp.dot(normed.T, grad_pre, preferred_element_type=jnp.float32)
    grad_normed = jnp.dot(grad_pre, w_proj.T, preferred_element_type=jnp.float32)
    grad_hidden = (cotangent.astype(jnp.float32) * loss_scale + norm_back(grad_normed)[0]).astype(
        jnp.bfloat16
    )
    grad_in = jnp.dot(embedded.T, grad_hidden, preferred_element_type=jnp.float32)
    grad_embedded = jnp.dot(grad_hidden, w_in.T, preferred_element_type=jnp.float32)
    slot_hot = (
        item_slot[:, None] == jnp.arange(fetched.shape[0], dtype=jnp.int32)[None, :]
    ).astype(jnp.float32)
    slot_grad = jnp.dot(slot_hot.T, grad_embedded, precision=lax.Precision.HIGHEST)
    action_grad = jnp.dot(
        action_hot.astype(jnp.float32).T, grad_embedded, precision=lax.Precision.HIGHEST
    )
    return ((grad_in, grad_proj, grad_out, action_grad), slot_grad)


CHUNKS = 4


def flip(axis, bit):
    at = lax.axis_index(axis)
    return jnp.bitwise_xor(at, 1 << bit), jnp.bitwise_and(at // (1 << bit), 1)


def combine_kernel(
    dp_bits,
    proj_ref,
    in_ref,
    out_ref,
    action_ref,
    slot_ref,
    proj_o,
    in_o,
    out_o,
    action_o,
    slot_o,
    work,
    final,
    action_acc,
    action_got,
    slot_got,
    *rest,
):
    got = rest[: dp_bits + 2]
    send_sem, recv_sem, gather_send, gather_recv, action_send, action_recv, slot_send, slot_recv = rest[
        dp_bits + 2 :
    ]
    chunks, _, rows, columns = work.shape
    table = lax.axis_index("table")
    other_table = 1 - table
    steps = [("rep", *flip("rep", 0)), ("table", *flip("table", 0))]
    steps += [("dp", *flip("dp", bit)) for bit in range(dp_bits)]

    barrier = pltpu.get_barrier_semaphore()
    for axis, partner, _ in steps:
        pl.semaphore_signal(
            barrier, inc=1, device_id={axis: partner}, device_id_type=pl.DeviceIdType.MESH
        )
    pl.semaphore_wait(barrier, len(steps))

    def remote(src, dst, send, recv, step):
        axis, partner, _ = steps[step]
        return pltpu.make_async_remote_copy(
            src_ref=src,
            dst_ref=dst,
            send_sem=send,
            recv_sem=recv,
            device_id={axis: partner},
            device_id_type=pl.DeviceIdType.MESH,
        )

    starts, counts = [0], [rows]
    sent = []
    halving = [0] + list(range(2, dp_bits + 2))
    for step in halving:
        half = counts[-1] // 2
        own = steps[step][2]
        sent.append(pl.multiple_of(starts[-1] + (1 - own) * half, 16))
        starts.append(pl.multiple_of(starts[-1] + own * half, 16))
        counts.append(half)

    slot_copy = remote(slot_ref.at[other_table], slot_got, slot_send, slot_recv, 1)
    slot_copy.start()
    action_acc[0] = action_ref[...]

    def action_copy(step):
        if step == 0:
            src, dst = action_acc.at[0], action_got.at[0]
        elif step == 1:
            src, dst = action_acc.at[1, other_table], action_got.at[1, 0]
        else:
            src, dst = action_acc.at[step, 0], action_got.at[step, 0]
        return remote(src, dst, action_send.at[step], action_recv.at[step], step)

    def action_add(step):
        if step == 0:
            action_acc[1] = action_acc[0] + action_got[0]
        elif step == 1:
            action_acc[2, 0] = action_acc[1, table] + action_got[1, 0]
        else:
            action_acc[step + 1, 0] = action_acc[step, 0] + action_got[step, 0]

    def reduce_copy(chunk, step):
        if step == 0:
            src = work.at[chunk, :, pl.ds(sent[0], counts[1])]
        elif step == 1:
            src = work.at[chunk, other_table, pl.ds(starts[1], counts[1])]
        else:
            src = work.at[chunk, table, pl.ds(sent[step - 1], counts[step])]
        return remote(
            src, got[step].at[chunk], send_sem.at[chunk, step], recv_sem.at[chunk, step], step
        )

    def reduce_add(chunk, step):
        part = max(step, 1)
        if step == 0:
            at = (chunk, slice(None), pl.ds(starts[1], counts[1]))
        else:
            at = (chunk, table, pl.ds(starts[part], counts[part]))
        total = work[at].astype(jnp.float32) + got[step][chunk].astype(jnp.float32)
        if step == dp_bits + 1:
            final[chunk, pl.ds(starts[part], counts[part])] = total.astype(jnp.bfloat16)
        else:
            work[at] = total.astype(jnp.bfloat16)

    backward = list(reversed(range(len(halving))))

    def gather_copy(chunk, place):
        at = backward[place]
        piece = final.at[chunk, pl.ds(starts[at + 1], counts[at + 1])]
        return remote(
            piece, piece, gather_send.at[chunk, place], gather_recv.at[chunk, place], halving[at]
        )

    reduces, gathers = len(steps), len(backward)
    half_proj, half_in, half_out = proj_ref.shape[0] // 2, in_ref.shape[0] // 2, out_ref.shape[0] // 2
    for chunk in range(chunks):
        wide = slice(chunk * columns, (chunk + 1) * columns)
        for side in range(2):
            work[chunk, side, :half_proj] = proj_ref[side * half_proj : (side + 1) * half_proj, wide]
            work[chunk, side, half_proj : half_proj + half_in] = in_ref[
                side * half_in : (side + 1) * half_in, wide
            ]
            work[chunk, side, half_proj + half_in :] = out_ref[
                side * half_out : (side + 1) * half_out, wide
            ]
        reduce_copy(chunk, 0).start()
    action_copy(0).start()

    for wave in range(chunks + reduces + gathers - 1):
        for chunk in range(chunks):
            at = wave - chunk
            if at < 0 or at >= reduces + gathers:
                continue
            if at < reduces:
                reduce_copy(chunk, at).wait_recv()
                reduce_add(chunk, at)
                if at + 1 < reduces:
                    reduce_copy(chunk, at + 1).start()
                else:
                    gather_copy(chunk, 0).start()
            else:
                place = at - reduces
                gather_copy(chunk, place).wait_recv()
                if place + 1 < gathers:
                    gather_copy(chunk, place + 1).start()
                else:
                    wide = slice(chunk * columns, (chunk + 1) * columns)
                    proj_o[:, wide] = final[chunk, :half_proj].astype(jnp.float32)
                    in_o[:, wide] = final[chunk, half_proj : half_proj + half_in].astype(jnp.float32)
                    out_o[:, wide] = final[chunk, half_proj + half_in :].astype(jnp.float32)
        if wave < reduces:
            action_copy(wave).wait_recv()
            action_add(wave)
            if wave + 1 < reduces:
                action_copy(wave + 1).start()

    action_o[...] = action_acc[reduces, 0]
    slot_copy.wait_recv()
    slot_o[table] = slot_ref[table]
    slot_o[other_table] = slot_got[...]
    slot_copy.wait_send()
    for step in range(reduces):
        action_copy(step).wait_send()
        for chunk in range(chunks):
            reduce_copy(chunk, step).wait_send()
    for place in range(gathers):
        for chunk in range(chunks):
            gather_copy(chunk, place).wait_send()


def combine(grad_proj, grad_in, grad_out, action_parts, slot_parts, dp_bits):
    wide = grad_proj.shape[1]
    rows = (grad_proj.shape[0] + grad_in.shape[0] + grad_out.shape[0]) // 2
    columns = wide // CHUNKS
    steps = dp_bits + 2
    _, actions, action_wide = action_parts.shape
    got = [pltpu.VMEM((CHUNKS, 2, rows // 2, columns), jnp.bfloat16)]
    got += [pltpu.VMEM((CHUNKS, rows // 2, columns), jnp.bfloat16)]
    got += [
        pltpu.VMEM((CHUNKS, rows >> (bit + 2), columns), jnp.bfloat16) for bit in range(dp_bits)
    ]
    dma = pltpu.SemaphoreType.DMA
    vmem = pl.BlockSpec(memory_space=pltpu.VMEM)
    return pl.pallas_call(
        lambda *refs: combine_kernel(dp_bits, *refs),
        out_shape=(
            jax.ShapeDtypeStruct((grad_proj.shape[0] // 2, wide), jnp.float32),
            jax.ShapeDtypeStruct((grad_in.shape[0] // 2, wide), jnp.float32),
            jax.ShapeDtypeStruct((grad_out.shape[0] // 2, wide), jnp.float32),
            jax.ShapeDtypeStruct((actions, action_wide), jnp.float32),
            jax.ShapeDtypeStruct(slot_parts.shape, jnp.float32),
        ),
        in_specs=[vmem] * 5,
        out_specs=(vmem,) * 5,
        scratch_shapes=[
            pltpu.VMEM((CHUNKS, 2, rows, columns), jnp.bfloat16),
            pltpu.VMEM((CHUNKS, rows, columns), jnp.bfloat16),
            pltpu.VMEM((steps + 1, 2, actions, action_wide), jnp.float32),
            pltpu.VMEM((steps, 2, actions, action_wide), jnp.float32),
            pltpu.VMEM(slot_parts.shape[1:], jnp.float32),
            *got,
            dma((CHUNKS, steps)),
            dma((CHUNKS, steps)),
            dma((CHUNKS, steps - 1)),
            dma((CHUNKS, steps - 1)),
            dma((steps,)),
            dma((steps,)),
            dma,
            dma,
        ],
        compiler_params=pltpu.CompilerParams(
            collective_id=0, has_side_effects=True, vmem_limit_bytes=40 * 2**20
        ),
    )(grad_proj, grad_in, grad_out, action_parts, slot_parts)


def shards(
    item_table,
    fetch_rows,
    fetch_count,
    item_slot,
    action_id,
    lengths,
    action_table,
    w_in,
    w_proj,
    w_out,
    cotangent,
):
    table_count = lax.axis_size("table")
    fetched_count = fetch_rows.shape[1]
    slot_count = fetched_count // table_count
    width = item_table.shape[1]
    valid = jnp.arange(slot_count, dtype=jnp.int32)[None, :] < fetch_count[0][:, None]
    taken = jnp.take(item_table, fetch_rows[0], axis=0).reshape(table_count, slot_count, width)
    outgoing = jnp.where(valid[:, :, None], taken, jnp.zeros_like(taken))
    fetched = lax.all_to_all(outgoing, "table", split_axis=0, concat_axis=0, tiled=True).reshape(
        fetched_count, width
    )
    dense, slot_grad = local_terms(
        fetched, item_slot, action_id, lengths[0], action_table, w_in, w_proj, w_out, cotangent
    )
    factor = (lax.axis_size("dp") * table_count * lax.axis_size("rep")) ** (-0.5)
    grad_in = dense[0] * factor
    grad_proj = dense[1] * factor
    grad_out = dense[2] * factor
    action_grad = dense[3] * factor
    dp_count = lax.axis_size("dp")
    dp_bits = dp_count.bit_length() - 1
    rows = (grad_in.shape[0] + grad_proj.shape[0] + grad_out.shape[0]) // 2
    pairs = table_count == 2 and lax.axis_size("rep") == 2 and dp_count == 1 << dp_bits
    if pairs and rows % (16 << (dp_bits + 1)) == 0:
        actions = action_grad.shape[0]
        proj_total, in_total, out_total, action_total, returned = combine(
            grad_proj.astype(jnp.bfloat16),
            grad_in.astype(jnp.bfloat16),
            grad_out.astype(jnp.bfloat16),
            action_grad.reshape(actions, 2, width // 2).swapaxes(0, 1),
            slot_grad.reshape(table_count, slot_count, width),
            dp_bits,
        )
        totals = (in_total, proj_total, out_total, action_total)
    else:
        returned = lax.all_to_all(
            slot_grad.reshape(table_count, slot_count, width),
            "table",
            split_axis=0,
            concat_axis=0,
            tiled=True,
        )
        shares = (
            lax.psum_scatter(grad_in, "table", scatter_dimension=0, tiled=True),
            lax.psum_scatter(grad_proj, "table", scatter_dimension=0, tiled=True),
            lax.psum_scatter(grad_out, "table", scatter_dimension=0, tiled=True),
            lax.psum_scatter(action_grad, "table", scatter_dimension=1, tiled=True),
        )
        totals = lax.psum((shares[0], shares[1], shares[2], shares[3]), ("dp", "rep"))
    returned = jnp.where(valid[:, :, None], returned, jnp.zeros_like(returned))
    item_grad = (
        jnp.zeros((item_table.shape[0], width), jnp.float32)
        .at[fetch_rows[0]]
        .add(returned.reshape(fetched_count, width))
    )
    return (item_grad, totals[0], totals[1], totals[2], totals[3])


def solution(mesh):
    return jax.shard_map(
        shards,
        mesh=mesh,
        in_specs=(
            P("table", None),
            P(("dp", "table", "rep"), None),
            P(("dp", "table", "rep"), None),
            P(("dp", "table", "rep")),
            P(("dp", "table", "rep")),
            P(("dp", "table", "rep"), None),
            P(),
            P(),
            P(),
            P(),
            P(("dp", "table", "rep"), None),
        ),
        out_specs=(
            P(("dp", "table", "rep"), None),
            P("table", None),
            P("table", None),
            P("table", None),
            P(None, "table"),
        ),
        check_vma=False,
    )
```

```python
import jax
import jax.numpy as jnp
from jax import lax
from jax.experimental import pallas as pl
from jax.experimental.pallas import tpu as pltpu
from jax.sharding import PartitionSpec as P

HEADS = 2
HEAD = 128


epsilon = 1e-05


def layer_norm(matrix):
    center = matrix - jnp.mean(matrix, axis=-1, keepdims=True)
    spread = jnp.mean(center * center, axis=-1, keepdims=True)
    return center * lax.rsqrt(spread + epsilon)


def sequence_layout(lengths, count):
    kinds = jnp.arange(lengths.shape[0], dtype=jnp.int32)
    ends = jnp.sum(
        jnp.where(kinds[None, :] <= kinds[:, None], lengths[None, :], 0), axis=1, dtype=jnp.int32
    )
    position = jnp.arange(count, dtype=jnp.int32)
    member = (position[:, None] < ends[None, :]) & (position[:, None] >= (ends - lengths)[None, :])
    row_length = jnp.sum(jnp.where(member, lengths[None, :], 0), axis=1, dtype=jnp.int32)
    first = jnp.sum(jnp.where(member, (ends - lengths)[None, :], 0), axis=1, dtype=jnp.int32)
    live = row_length > 0
    allowed = (position[None, :] >= first[:, None]) & (position[None, :] <= position[:, None])
    allowed = allowed & live[:, None]
    safe_length = jnp.maximum(row_length, 1).astype(jnp.float32)
    inverse_length = jnp.where(live, 1.0 / safe_length, jnp.zeros_like(safe_length))
    return (allowed, inverse_length, live)


def mixing(projected, allowed, inverse_length, heads, head):
    width = heads * head
    count = projected.shape[0]
    activated = jax.nn.silu(projected)
    gating = activated[:, :width].astype(jnp.bfloat16)
    value_rows = activated[:, width : 2 * width].astype(jnp.bfloat16)
    queries = activated[:, 2 * width : 3 * width].astype(jnp.bfloat16)
    key_rows = activated[:, 3 * width :].astype(jnp.bfloat16)
    query_heads = queries.reshape(count, heads, head)
    key_heads = key_rows.reshape(count, heads, head)
    value_heads = value_rows.reshape(count, heads, head)
    scores = jnp.einsum(
        "thd,shd->hts", query_heads, key_heads, preferred_element_type=jnp.float32
    ) * head ** (-0.5)
    weights = jnp.where(allowed[None], jax.nn.silu(scores), 0.0) * inverse_length[None, :, None]
    weights = weights.astype(jnp.bfloat16)
    attended = jnp.einsum(
        "hts,shd->thd", weights, value_heads, preferred_element_type=jnp.float32
    ).reshape(count, width)
    return (layer_norm(attended) * gating.astype(jnp.float32)).astype(jnp.bfloat16)


def local_terms(
    fetched, item_slot, action_id, lengths, action_table, w_in, w_proj, w_out, cotangent
):
    count = cotangent.shape[0]
    loss_scale = count ** (-0.5)
    allowed, inverse_length, live = sequence_layout(lengths, count)
    cotangent = jnp.where(live[:, None], cotangent, jnp.zeros_like(cotangent))
    item_hot = item_slot[:, None] == jnp.arange(fetched.shape[0], dtype=jnp.int32)[None, :]
    item_rows = jnp.dot(item_hot.astype(jnp.bfloat16), fetched, preferred_element_type=jnp.float32)
    action_hot = action_id[:, None] == jnp.arange(action_table.shape[0], dtype=jnp.int32)[None, :]
    action_rows = jnp.dot(
        action_hot.astype(jnp.bfloat16), action_table, preferred_element_type=jnp.float32
    )
    embedded = (item_rows + action_rows).astype(jnp.bfloat16)
    hidden = jnp.dot(embedded, w_in, preferred_element_type=jnp.float32)
    normed_full, norm_back = jax.vjp(layer_norm, hidden)
    normed = normed_full.astype(jnp.bfloat16)
    projected = jnp.dot(normed, w_proj, preferred_element_type=jnp.float32)
    mixed_rows, mix_back = jax.vjp(
        lambda values: mixing(values, allowed, inverse_length, HEADS, HEAD), projected
    )
    grad_out = jnp.dot(mixed_rows.T, cotangent, preferred_element_type=jnp.float32) * loss_scale
    grad_mixed = (
        jnp.dot(cotangent, w_out.T, preferred_element_type=jnp.float32) * loss_scale
    ).astype(jnp.bfloat16)
    grad_pre = mix_back(grad_mixed)[0].astype(jnp.bfloat16)
    grad_proj = jnp.dot(normed.T, grad_pre, preferred_element_type=jnp.float32)
    grad_normed = jnp.dot(grad_pre, w_proj.T, preferred_element_type=jnp.float32)
    grad_hidden = (cotangent.astype(jnp.float32) * loss_scale + norm_back(grad_normed)[0]).astype(
        jnp.bfloat16
    )
    grad_in = jnp.dot(embedded.T, grad_hidden, preferred_element_type=jnp.float32)
    grad_embedded = jnp.dot(grad_hidden, w_in.T, preferred_element_type=jnp.float32)
    slot_hot = (
        item_slot[:, None] == jnp.arange(fetched.shape[0], dtype=jnp.int32)[None, :]
    ).astype(jnp.float32)
    slot_grad = jnp.dot(slot_hot.T, grad_embedded, precision=lax.Precision.HIGHEST)
    action_grad = jnp.dot(
        action_hot.astype(jnp.float32).T, grad_embedded, precision=lax.Precision.HIGHEST
    )
    return ((grad_in, grad_proj, grad_out, action_grad), slot_grad)


CHUNKS = 4


def flip(axis, bit):
    at = lax.axis_index(axis)
    return jnp.bitwise_xor(at, 1 << bit), jnp.bitwise_and(at // (1 << bit), 1)


def combine_kernel(
    dp_bits,
    proj_ref,
    in_ref,
    out_ref,
    action_ref,
    slot_ref,
    proj_o,
    in_o,
    out_o,
    action_o,
    slot_o,
    work,
    final,
    action_acc,
    action_got,
    slot_got,
    *rest,
):
    got = rest[:4]
    send_sem, recv_sem, gather_send, gather_recv, action_send, action_recv, slot_send, slot_recv = rest[
        4:12
    ]
    line_send, line_recv, line_back_send, line_back_recv = rest[12:]
    chunks, _, rows, columns = work.shape
    table = lax.axis_index("table")
    other_table = 1 - table
    steps = [("rep", *flip("rep", 0)), ("table", *flip("table", 0))]
    steps += [("dp", *flip("dp", bit)) for bit in range(dp_bits)]

    line = (1 << dp_bits) // 2
    place_in_line = lax.axis_index("dp") // 2
    low = lax.axis_index("dp") % 2

    def line_place(offset):
        return (place_in_line + offset) % line

    barrier = pltpu.get_barrier_semaphore()
    peers = [{axis: partner} for axis, partner, _ in steps[:3]]
    peers += [{"dp": line_place(offset) * 2 + low} for offset in range(1, line)]
    for peer in peers:
        pl.semaphore_signal(barrier, inc=1, device_id=peer, device_id_type=pl.DeviceIdType.MESH)
    pl.semaphore_wait(barrier, len(peers))

    def remote(src, dst, send, recv, step):
        axis, partner, _ = steps[step]
        return pltpu.make_async_remote_copy(
            src_ref=src,
            dst_ref=dst,
            send_sem=send,
            recv_sem=recv,
            device_id={axis: partner},
            device_id_type=pl.DeviceIdType.MESH,
        )

    starts, counts = [0], [rows]
    sent = []
    halving = [0, 2]
    for step in halving:
        half = counts[-1] // 2
        own = steps[step][2]
        sent.append(pl.multiple_of(starts[-1] + (1 - own) * half, 16))
        starts.append(pl.multiple_of(starts[-1] + own * half, 16))
        counts.append(half)

    slot_copy = remote(slot_ref.at[other_table], slot_got, slot_send, slot_recv, 1)
    slot_copy.start()
    action_acc[0] = action_ref[...]

    def action_copy(step):
        if step == 0:
            src, dst = action_acc.at[0], action_got.at[0]
        elif step == 1:
            src, dst = action_acc.at[1, other_table], action_got.at[1, 0]
        else:
            src, dst = action_acc.at[step, 0], action_got.at[step, 0]
        return remote(src, dst, action_send.at[step], action_recv.at[step], step)

    def action_add(step):
        if step == 0:
            action_acc[1] = action_acc[0] + action_got[0]
        elif step == 1:
            action_acc[2, 0] = action_acc[1, table] + action_got[1, 0]
        else:
            action_acc[step + 1, 0] = action_acc[step, 0] + action_got[step, 0]

    piece = counts[2] // line

    def piece_at(place):
        return pl.ds(pl.multiple_of(starts[2] + place * piece, 16), piece)

    def line_copy(chunk, offset, back):
        target = line_place(offset)
        if back:
            src = dst = final.at[chunk, piece_at(place_in_line)]
            sems = line_back_send.at[chunk, offset - 1], line_back_recv.at[chunk, offset - 1]
        else:
            src = work.at[chunk, table, piece_at(target)]
            dst = got[3].at[chunk, offset - 1]
            sems = line_send.at[chunk, offset - 1], line_recv.at[chunk, offset - 1]
        return pltpu.make_async_remote_copy(
            src_ref=src,
            dst_ref=dst,
            send_sem=sems[0],
            recv_sem=sems[1],
            device_id={"dp": target * 2 + low},
            device_id_type=pl.DeviceIdType.MESH,
        )

    offsets = sorted(range(1, line), key=lambda offset: -min(offset, line - offset))

    def reduce_copies(chunk, step):
        if step == 0:
            src = work.at[chunk, :, pl.ds(sent[0], counts[1])]
        elif step == 1:
            src = work.at[chunk, other_table, pl.ds(starts[1], counts[1])]
        elif step == 2:
            src = work.at[chunk, table, pl.ds(sent[1], counts[2])]
        else:
            return [line_copy(chunk, offset, False) for offset in offsets]
        sems = send_sem.at[chunk, step], recv_sem.at[chunk, step]
        return [remote(src, got[step].at[chunk], *sems, step)]

    def reduce_add(chunk, step):
        if step == 0:
            at = (chunk, slice(None), pl.ds(starts[1], counts[1]))
        elif step < 3:
            at = (chunk, table, pl.ds(starts[step], counts[step]))
        else:
            total = work[chunk, table, piece_at(place_in_line)].astype(jnp.float32)
            for offset in range(1, line):
                total += got[3][chunk, offset - 1].astype(jnp.float32)
            final[chunk, piece_at(place_in_line)] = total.astype(jnp.bfloat16)
            return
        total = work[at].astype(jnp.float32) + got[step][chunk].astype(jnp.float32)
        work[at] = total.astype(jnp.bfloat16)

    def gather_copies(chunk, place):
        if place == 0:
            return [line_copy(chunk, offset, True) for offset in offsets]
        at = 2 - place
        part = final.at[chunk, pl.ds(starts[at + 1], counts[at + 1])]
        sems = gather_send.at[chunk, place - 1], gather_recv.at[chunk, place - 1]
        return [remote(part, part, *sems, halving[at])]

    def start(copies):
        for copy in copies:
            copy.start()

    def received(copies):
        for copy in copies:
            copy.wait_recv()

    reduces, gathers, action_steps = 4, 3, len(steps)
    half_proj, half_in, half_out = proj_ref.shape[0] // 2, in_ref.shape[0] // 2, out_ref.shape[0] // 2
    for chunk in range(chunks):
        wide = slice(chunk * columns, (chunk + 1) * columns)
        for side in range(2):
            work[chunk, side, :half_proj] = proj_ref[side * half_proj : (side + 1) * half_proj, wide]
            work[chunk, side, half_proj : half_proj + half_in] = in_ref[
                side * half_in : (side + 1) * half_in, wide
            ]
            work[chunk, side, half_proj + half_in :] = out_ref[
                side * half_out : (side + 1) * half_out, wide
            ]
        start(reduce_copies(chunk, 0))
    action_copy(0).start()

    for wave in range(chunks + reduces + gathers - 1):
        for chunk in range(chunks):
            at = wave - chunk
            if at < 0 or at >= reduces + gathers:
                continue
            if at < reduces:
                received(reduce_copies(chunk, at))
                reduce_add(chunk, at)
                if at + 1 < reduces:
                    start(reduce_copies(chunk, at + 1))
                else:
                    start(gather_copies(chunk, 0))
            else:
                place = at - reduces
                received(gather_copies(chunk, place))
                if place + 1 < gathers:
                    start(gather_copies(chunk, place + 1))
                else:
                    wide = slice(chunk * columns, (chunk + 1) * columns)
                    proj_o[:, wide] = final[chunk, :half_proj]
                    in_o[:, wide] = final[chunk, half_proj : half_proj + half_in]
                    out_o[:, wide] = final[chunk, half_proj + half_in :]
        if wave < action_steps:
            action_copy(wave).wait_recv()
            action_add(wave)
            if wave + 1 < action_steps:
                action_copy(wave + 1).start()

    action_o[...] = action_acc[action_steps, 0]
    slot_copy.wait_recv()
    slot_o[table] = slot_ref[table]
    slot_o[other_table] = slot_got[...]
    slot_copy.wait_send()
    for step in range(action_steps):
        action_copy(step).wait_send()
    for chunk in range(chunks):
        for step in range(reduces):
            for copy in reduce_copies(chunk, step):
                copy.wait_send()
        for place in range(gathers):
            for copy in gather_copies(chunk, place):
                copy.wait_send()


def combine(grad_proj, grad_in, grad_out, action_parts, slot_parts, dp_bits):
    wide = grad_proj.shape[1]
    rows = (grad_proj.shape[0] + grad_in.shape[0] + grad_out.shape[0]) // 2
    columns = wide // CHUNKS
    steps = dp_bits + 2
    _, actions, action_wide = action_parts.shape
    got = [pltpu.VMEM((CHUNKS, 2, rows // 2, columns), jnp.bfloat16)]
    got += [pltpu.VMEM((CHUNKS, rows // 2, columns), jnp.bfloat16)]
    got += [pltpu.VMEM((CHUNKS, rows // 4, columns), jnp.bfloat16)]
    line = (1 << dp_bits) // 2
    got += [pltpu.VMEM((CHUNKS, line - 1, rows // 4 // line, columns), jnp.bfloat16)]
    dma = pltpu.SemaphoreType.DMA
    vmem = pl.BlockSpec(memory_space=pltpu.VMEM)
    return pl.pallas_call(
        lambda *refs: combine_kernel(dp_bits, *refs),
        out_shape=(
            jax.ShapeDtypeStruct((grad_proj.shape[0] // 2, wide), jnp.bfloat16),
            jax.ShapeDtypeStruct((grad_in.shape[0] // 2, wide), jnp.bfloat16),
            jax.ShapeDtypeStruct((grad_out.shape[0] // 2, wide), jnp.bfloat16),
            jax.ShapeDtypeStruct((actions, action_wide), jnp.float32),
            jax.ShapeDtypeStruct(slot_parts.shape, jnp.float32),
        ),
        in_specs=[vmem] * 5,
        out_specs=(vmem,) * 5,
        scratch_shapes=[
            pltpu.VMEM((CHUNKS, 2, rows, columns), jnp.bfloat16),
            pltpu.VMEM((CHUNKS, rows, columns), jnp.bfloat16),
            pltpu.VMEM((steps + 1, 2, actions, action_wide), jnp.float32),
            pltpu.VMEM((steps, 2, actions, action_wide), jnp.float32),
            pltpu.VMEM(slot_parts.shape[1:], jnp.float32),
            *got,
            dma((CHUNKS, 3)),
            dma((CHUNKS, 3)),
            dma((CHUNKS, 2)),
            dma((CHUNKS, 2)),
            dma((steps,)),
            dma((steps,)),
            dma,
            dma,
            *[dma((CHUNKS, line - 1))] * 4,
        ],
        compiler_params=pltpu.CompilerParams(
            collective_id=0, has_side_effects=True, vmem_limit_bytes=40 * 2**20
        ),
    )(grad_proj, grad_in, grad_out, action_parts, slot_parts)


def shards(
    item_table,
    fetch_rows,
    fetch_count,
    item_slot,
    action_id,
    lengths,
    action_table,
    w_in,
    w_proj,
    w_out,
    cotangent,
):
    table_count = lax.axis_size("table")
    fetched_count = fetch_rows.shape[1]
    slot_count = fetched_count // table_count
    width = item_table.shape[1]
    valid = jnp.arange(slot_count, dtype=jnp.int32)[None, :] < fetch_count[0][:, None]
    rows_at = jnp.arange(item_table.shape[0], dtype=jnp.int32)
    fetch_hot = (fetch_rows[0][:, None] == rows_at[None, :]) & valid.reshape(fetched_count, 1)
    outgoing = jnp.dot(
        fetch_hot.astype(jnp.bfloat16), item_table, preferred_element_type=jnp.float32
    ).astype(jnp.bfloat16)
    outgoing = outgoing.reshape(table_count, slot_count, width)
    if table_count == 2:
        first = lax.axis_index("table") == 0
        own = jnp.where(first, outgoing[0], outgoing[1])
        asked = jnp.where(first, outgoing[1], outgoing[0])
        came = lax.ppermute(asked, "table", [(0, 1), (1, 0)])
        fetched = jnp.concatenate([jnp.where(first, own, came), jnp.where(first, came, own)])
    else:
        fetched = lax.all_to_all(outgoing, "table", split_axis=0, concat_axis=0, tiled=True).reshape(
            fetched_count, width
        )
    dense, slot_grad = local_terms(
        fetched, item_slot, action_id, lengths[0], action_table, w_in, w_proj, w_out, cotangent
    )
    factor = (lax.axis_size("dp") * table_count * lax.axis_size("rep")) ** (-0.5)
    grad_in = dense[0] * factor
    grad_proj = dense[1] * factor
    grad_out = dense[2] * factor
    action_grad = dense[3] * factor
    dp_count = lax.axis_size("dp")
    dp_bits = dp_count.bit_length() - 1
    rows = (grad_in.shape[0] + grad_proj.shape[0] + grad_out.shape[0]) // 2
    pairs = table_count == 2 and lax.axis_size("rep") == 2 and dp_count == 1 << dp_bits
    pairs = pairs and dp_bits > 1
    if pairs and rows % (16 << (dp_bits + 1)) == 0:
        actions = action_grad.shape[0]
        proj_total, in_total, out_total, action_total, returned = combine(
            grad_proj.astype(jnp.bfloat16),
            grad_in.astype(jnp.bfloat16),
            grad_out.astype(jnp.bfloat16),
            action_grad.reshape(actions, 2, width // 2).swapaxes(0, 1),
            slot_grad.reshape(table_count, slot_count, width),
            dp_bits,
        )
        totals = (
            in_total.astype(jnp.float32),
            proj_total.astype(jnp.float32),
            out_total.astype(jnp.float32),
            action_total,
        )
    else:
        returned = lax.all_to_all(
            slot_grad.reshape(table_count, slot_count, width),
            "table",
            split_axis=0,
            concat_axis=0,
            tiled=True,
        )
        shares = (
            lax.psum_scatter(grad_in, "table", scatter_dimension=0, tiled=True),
            lax.psum_scatter(grad_proj, "table", scatter_dimension=0, tiled=True),
            lax.psum_scatter(grad_out, "table", scatter_dimension=0, tiled=True),
            lax.psum_scatter(action_grad, "table", scatter_dimension=1, tiled=True),
        )
        totals = lax.psum((shares[0], shares[1], shares[2], shares[3]), ("dp", "rep"))
    item_grad = jnp.dot(
        fetch_hot.astype(jnp.float32).T,
        returned.reshape(fetched_count, width),
        precision=lax.Precision.HIGHEST,
    )
    return (item_grad, totals[0], totals[1], totals[2], totals[3])


def solution(mesh):
    return jax.shard_map(
        shards,
        mesh=mesh,
        in_specs=(
            P("table", None),
            P(("dp", "table", "rep"), None),
            P(("dp", "table", "rep"), None),
            P(("dp", "table", "rep")),
            P(("dp", "table", "rep")),
            P(("dp", "table", "rep"), None),
            P(),
            P(),
            P(),
            P(),
            P(("dp", "table", "rep"), None),
        ),
        out_specs=(
            P(("dp", "table", "rep"), None),
            P("table", None),
            P("table", None),
            P("table", None),
            P(None, "table"),
        ),
        check_vma=False,
    )
```

```python
import jax
import jax.numpy as jnp
from jax import lax
from jax.experimental import pallas as pl
from jax.experimental.pallas import tpu as pltpu
from jax.sharding import PartitionSpec as P

HEADS = 2
HEAD = 128


epsilon = 1e-05


def layer_norm(matrix):
    center = matrix - jnp.mean(matrix, axis=-1, keepdims=True)
    spread = jnp.mean(center * center, axis=-1, keepdims=True)
    return center * lax.rsqrt(spread + epsilon)


def sequence_layout(lengths, count):
    kinds = jnp.arange(lengths.shape[0], dtype=jnp.int32)
    ends = jnp.sum(
        jnp.where(kinds[None, :] <= kinds[:, None], lengths[None, :], 0), axis=1, dtype=jnp.int32
    )
    position = jnp.arange(count, dtype=jnp.int32)
    member = (position[:, None] < ends[None, :]) & (position[:, None] >= (ends - lengths)[None, :])
    row_length = jnp.sum(jnp.where(member, lengths[None, :], 0), axis=1, dtype=jnp.int32)
    first = jnp.sum(jnp.where(member, (ends - lengths)[None, :], 0), axis=1, dtype=jnp.int32)
    live = row_length > 0
    allowed = (position[None, :] >= first[:, None]) & (position[None, :] <= position[:, None])
    allowed = allowed & live[:, None]
    safe_length = jnp.maximum(row_length, 1).astype(jnp.float32)
    inverse_length = jnp.where(live, 1.0 / safe_length, jnp.zeros_like(safe_length))
    return (allowed, inverse_length, live)


def mixing(projected, allowed, inverse_length, heads, head):
    width = heads * head
    count = projected.shape[0]
    activated = jax.nn.silu(projected)
    gating = activated[:, :width].astype(jnp.bfloat16)
    value_rows = activated[:, width : 2 * width].astype(jnp.bfloat16)
    queries = activated[:, 2 * width : 3 * width].astype(jnp.bfloat16)
    key_rows = activated[:, 3 * width :].astype(jnp.bfloat16)
    query_heads = queries.reshape(count, heads, head)
    key_heads = key_rows.reshape(count, heads, head)
    value_heads = value_rows.reshape(count, heads, head)
    scores = jnp.einsum(
        "thd,shd->hts", query_heads, key_heads, preferred_element_type=jnp.float32
    ) * head ** (-0.5)
    weights = jnp.where(allowed[None], jax.nn.silu(scores), 0.0) * inverse_length[None, :, None]
    weights = weights.astype(jnp.bfloat16)
    attended = jnp.einsum(
        "hts,shd->thd", weights, value_heads, preferred_element_type=jnp.float32
    ).reshape(count, width)
    return (layer_norm(attended) * gating.astype(jnp.float32)).astype(jnp.bfloat16)


def local_terms(
    fetched, item_slot, action_id, lengths, action_table, w_in, w_proj, w_out, cotangent
):
    count = cotangent.shape[0]
    loss_scale = count ** (-0.5)
    allowed, inverse_length, live = sequence_layout(lengths, count)
    cotangent = jnp.where(live[:, None], cotangent, jnp.zeros_like(cotangent))
    item_hot = item_slot[:, None] == jnp.arange(fetched.shape[0], dtype=jnp.int32)[None, :]
    item_rows = jnp.dot(item_hot.astype(jnp.bfloat16), fetched, preferred_element_type=jnp.float32)
    action_hot = action_id[:, None] == jnp.arange(action_table.shape[0], dtype=jnp.int32)[None, :]
    action_rows = jnp.dot(
        action_hot.astype(jnp.bfloat16), action_table, preferred_element_type=jnp.float32
    )
    embedded = (item_rows + action_rows).astype(jnp.bfloat16)
    hidden = jnp.dot(embedded, w_in, preferred_element_type=jnp.float32)
    normed_full, norm_back = jax.vjp(layer_norm, hidden)
    normed = normed_full.astype(jnp.bfloat16)
    projected = jnp.dot(normed, w_proj, preferred_element_type=jnp.float32)
    mixed_rows, mix_back = jax.vjp(
        lambda values: mixing(values, allowed, inverse_length, HEADS, HEAD), projected
    )
    grad_out = jnp.dot(mixed_rows.T, cotangent, preferred_element_type=jnp.float32) * loss_scale
    grad_mixed = (
        jnp.dot(cotangent, w_out.T, preferred_element_type=jnp.float32) * loss_scale
    ).astype(jnp.bfloat16)
    grad_pre = mix_back(grad_mixed)[0].astype(jnp.bfloat16)
    grad_proj = jnp.dot(normed.T, grad_pre, preferred_element_type=jnp.float32)
    grad_normed = jnp.dot(grad_pre, w_proj.T, preferred_element_type=jnp.float32)
    grad_hidden = (cotangent.astype(jnp.float32) * loss_scale + norm_back(grad_normed)[0]).astype(
        jnp.bfloat16
    )
    grad_in = jnp.dot(embedded.T, grad_hidden, preferred_element_type=jnp.float32)
    grad_embedded = jnp.dot(grad_hidden, w_in.T, preferred_element_type=jnp.float32)
    slot_hot = (
        item_slot[:, None] == jnp.arange(fetched.shape[0], dtype=jnp.int32)[None, :]
    ).astype(jnp.float32)
    slot_grad = jnp.dot(slot_hot.T, grad_embedded, precision=lax.Precision.HIGH)
    action_grad = jnp.dot(
        action_hot.astype(jnp.float32).T, grad_embedded, precision=lax.Precision.HIGH
    )
    return ((grad_in, grad_proj, grad_out, action_grad), slot_grad)


CHUNKS = 4


def flip(axis, bit):
    at = lax.axis_index(axis)
    return jnp.bitwise_xor(at, 1 << bit), jnp.bitwise_and(at // (1 << bit), 1)


def combine_kernel(
    dp_bits,
    proj_ref,
    in_ref,
    out_ref,
    action_ref,
    slot_ref,
    proj_o,
    in_o,
    out_o,
    action_o,
    slot_o,
    work,
    final,
    action_acc,
    action_got,
    slot_got,
    *rest,
):
    got = rest[:4]
    send_sem, recv_sem, gather_send, gather_recv, action_send, action_recv, slot_send, slot_recv = rest[
        4:12
    ]
    line_send, line_recv, line_back_send, line_back_recv = rest[12:]
    chunks, _, rows, columns = work.shape
    table = lax.axis_index("table")
    other_table = 1 - table
    steps = [("rep", *flip("rep", 0)), ("table", *flip("table", 0))]
    steps += [("dp", *flip("dp", bit)) for bit in range(dp_bits)]

    line = (1 << dp_bits) // 2
    place_in_line = lax.axis_index("dp") // 2
    low = lax.axis_index("dp") % 2

    def line_place(offset):
        return (place_in_line + offset) % line

    barrier = pltpu.get_barrier_semaphore()
    peers = [{axis: partner} for axis, partner, _ in steps[:3]]
    peers += [{"dp": line_place(offset) * 2 + low} for offset in range(1, line)]
    for peer in peers:
        pl.semaphore_signal(barrier, inc=1, device_id=peer, device_id_type=pl.DeviceIdType.MESH)
    pl.semaphore_wait(barrier, len(peers))

    def remote(src, dst, send, recv, step):
        axis, partner, _ = steps[step]
        return pltpu.make_async_remote_copy(
            src_ref=src,
            dst_ref=dst,
            send_sem=send,
            recv_sem=recv,
            device_id={axis: partner},
            device_id_type=pl.DeviceIdType.MESH,
        )

    starts, counts = [0], [rows]
    sent = []
    halving = [0, 2]
    for step in halving:
        half = counts[-1] // 2
        own = steps[step][2]
        sent.append(pl.multiple_of(starts[-1] + (1 - own) * half, 16))
        starts.append(pl.multiple_of(starts[-1] + own * half, 16))
        counts.append(half)

    slot_copy = remote(slot_ref.at[other_table], slot_got, slot_send, slot_recv, 1)
    slot_copy.start()
    action_acc[0] = action_ref[...]

    def action_copy(step):
        if step == 0:
            src, dst = action_acc.at[0], action_got.at[0]
        elif step == 1:
            src, dst = action_acc.at[1, other_table], action_got.at[1, 0]
        else:
            src, dst = action_acc.at[step, 0], action_got.at[step, 0]
        return remote(src, dst, action_send.at[step], action_recv.at[step], step)

    def action_add(step):
        if step == 0:
            action_acc[1] = action_acc[0] + action_got[0]
        elif step == 1:
            action_acc[2, 0] = action_acc[1, table] + action_got[1, 0]
        else:
            action_acc[step + 1, 0] = action_acc[step, 0] + action_got[step, 0]

    piece = counts[2] // line

    def piece_at(place):
        return pl.ds(pl.multiple_of(starts[2] + place * piece, 16), piece)

    def line_copy(chunk, offset, back):
        target = line_place(offset)
        if back:
            src = dst = final.at[chunk, piece_at(place_in_line)]
            sems = line_back_send.at[chunk, offset - 1], line_back_recv.at[chunk, offset - 1]
        else:
            src = work.at[chunk, table, piece_at(target)]
            dst = got[3].at[chunk, offset - 1]
            sems = line_send.at[chunk, offset - 1], line_recv.at[chunk, offset - 1]
        return pltpu.make_async_remote_copy(
            src_ref=src,
            dst_ref=dst,
            send_sem=sems[0],
            recv_sem=sems[1],
            device_id={"dp": target * 2 + low},
            device_id_type=pl.DeviceIdType.MESH,
        )

    offsets = sorted(range(1, line), key=lambda offset: -min(offset, line - offset))

    def reduce_copies(chunk, step):
        if step == 0:
            src = work.at[chunk, :, pl.ds(sent[0], counts[1])]
        elif step == 1:
            src = work.at[chunk, other_table, pl.ds(starts[1], counts[1])]
        elif step == 2:
            src = work.at[chunk, table, pl.ds(sent[1], counts[2])]
        else:
            return [line_copy(chunk, offset, False) for offset in offsets]
        sems = send_sem.at[chunk, step], recv_sem.at[chunk, step]
        return [remote(src, got[step].at[chunk], *sems, step)]

    def reduce_add(chunk, step):
        if step == 0:
            at = (chunk, slice(None), pl.ds(starts[1], counts[1]))
        elif step < 3:
            at = (chunk, table, pl.ds(starts[step], counts[step]))
        else:
            total = work[chunk, table, piece_at(place_in_line)].astype(jnp.float32)
            for offset in range(1, line):
                total += got[3][chunk, offset - 1].astype(jnp.float32)
            final[chunk, piece_at(place_in_line)] = total.astype(jnp.bfloat16)
            return
        total = work[at].astype(jnp.float32) + got[step][chunk].astype(jnp.float32)
        work[at] = total.astype(jnp.bfloat16)

    def gather_copies(chunk, place):
        if place == 0:
            return [line_copy(chunk, offset, True) for offset in offsets]
        at = 2 - place
        part = final.at[chunk, pl.ds(starts[at + 1], counts[at + 1])]
        sems = gather_send.at[chunk, place - 1], gather_recv.at[chunk, place - 1]
        return [remote(part, part, *sems, halving[at])]

    def start(copies):
        for copy in copies:
            copy.start()

    def received(copies):
        for copy in copies:
            copy.wait_recv()

    reduces, gathers, action_steps = 4, 3, len(steps)
    half_proj, half_in, half_out = proj_ref.shape[0] // 2, in_ref.shape[0] // 2, out_ref.shape[0] // 2
    for chunk in range(chunks):
        wide = slice(chunk * columns, (chunk + 1) * columns)
        for side in range(2):
            work[chunk, side, :half_proj] = proj_ref[side * half_proj : (side + 1) * half_proj, wide]
            work[chunk, side, half_proj : half_proj + half_in] = in_ref[
                side * half_in : (side + 1) * half_in, wide
            ]
            work[chunk, side, half_proj + half_in :] = out_ref[
                side * half_out : (side + 1) * half_out, wide
            ]
        start(reduce_copies(chunk, 0))
    action_copy(0).start()

    for wave in range(chunks + reduces + gathers - 1):
        for chunk in range(chunks):
            at = wave - chunk
            if at < 0 or at >= reduces + gathers:
                continue
            if at < reduces:
                received(reduce_copies(chunk, at))
                reduce_add(chunk, at)
                if at + 1 < reduces:
                    start(reduce_copies(chunk, at + 1))
                else:
                    start(gather_copies(chunk, 0))
            else:
                place = at - reduces
                received(gather_copies(chunk, place))
                if place + 1 < gathers:
                    start(gather_copies(chunk, place + 1))
                else:
                    wide = slice(chunk * columns, (chunk + 1) * columns)
                    proj_o[:, wide] = final[chunk, :half_proj]
                    in_o[:, wide] = final[chunk, half_proj : half_proj + half_in]
                    out_o[:, wide] = final[chunk, half_proj + half_in :]
        if wave < action_steps:
            action_copy(wave).wait_recv()
            action_add(wave)
            if wave + 1 < action_steps:
                action_copy(wave + 1).start()

    action_o[...] = action_acc[action_steps, 0]
    slot_copy.wait_recv()
    slot_o[table] = slot_ref[table]
    slot_o[other_table] = slot_got[...]
    slot_copy.wait_send()
    for step in range(action_steps):
        action_copy(step).wait_send()
    for chunk in range(chunks):
        for step in range(reduces):
            for copy in reduce_copies(chunk, step):
                copy.wait_send()
        for place in range(gathers):
            for copy in gather_copies(chunk, place):
                copy.wait_send()


def combine(grad_proj, grad_in, grad_out, action_parts, slot_parts, dp_bits):
    wide = grad_proj.shape[1]
    rows = (grad_proj.shape[0] + grad_in.shape[0] + grad_out.shape[0]) // 2
    columns = wide // CHUNKS
    steps = dp_bits + 2
    _, actions, action_wide = action_parts.shape
    got = [pltpu.VMEM((CHUNKS, 2, rows // 2, columns), jnp.bfloat16)]
    got += [pltpu.VMEM((CHUNKS, rows // 2, columns), jnp.bfloat16)]
    got += [pltpu.VMEM((CHUNKS, rows // 4, columns), jnp.bfloat16)]
    line = (1 << dp_bits) // 2
    got += [pltpu.VMEM((CHUNKS, line - 1, rows // 4 // line, columns), jnp.bfloat16)]
    dma = pltpu.SemaphoreType.DMA
    vmem = pl.BlockSpec(memory_space=pltpu.VMEM)
    return pl.pallas_call(
        lambda *refs: combine_kernel(dp_bits, *refs),
        out_shape=(
            jax.ShapeDtypeStruct((grad_proj.shape[0] // 2, wide), jnp.bfloat16),
            jax.ShapeDtypeStruct((grad_in.shape[0] // 2, wide), jnp.bfloat16),
            jax.ShapeDtypeStruct((grad_out.shape[0] // 2, wide), jnp.bfloat16),
            jax.ShapeDtypeStruct((actions, action_wide), jnp.float32),
            jax.ShapeDtypeStruct(slot_parts.shape, jnp.float32),
        ),
        in_specs=[vmem] * 5,
        out_specs=(vmem,) * 5,
        scratch_shapes=[
            pltpu.VMEM((CHUNKS, 2, rows, columns), jnp.bfloat16),
            pltpu.VMEM((CHUNKS, rows, columns), jnp.bfloat16),
            pltpu.VMEM((steps + 1, 2, actions, action_wide), jnp.float32),
            pltpu.VMEM((steps, 2, actions, action_wide), jnp.float32),
            pltpu.VMEM(slot_parts.shape[1:], jnp.float32),
            *got,
            dma((CHUNKS, 3)),
            dma((CHUNKS, 3)),
            dma((CHUNKS, 2)),
            dma((CHUNKS, 2)),
            dma((steps,)),
            dma((steps,)),
            dma,
            dma,
            *[dma((CHUNKS, line - 1))] * 4,
        ],
        compiler_params=pltpu.CompilerParams(
            collective_id=0, has_side_effects=True, vmem_limit_bytes=40 * 2**20
        ),
    )(grad_proj, grad_in, grad_out, action_parts, slot_parts)


def shards(
    item_table,
    fetch_rows,
    fetch_count,
    item_slot,
    action_id,
    lengths,
    action_table,
    w_in,
    w_proj,
    w_out,
    cotangent,
):
    table_count = lax.axis_size("table")
    fetched_count = fetch_rows.shape[1]
    slot_count = fetched_count // table_count
    width = item_table.shape[1]
    valid = jnp.arange(slot_count, dtype=jnp.int32)[None, :] < fetch_count[0][:, None]
    rows_at = jnp.arange(item_table.shape[0], dtype=jnp.int32)
    fetch_hot = (fetch_rows[0][:, None] == rows_at[None, :]) & valid.reshape(fetched_count, 1)
    outgoing = jnp.dot(
        fetch_hot.astype(jnp.bfloat16), item_table, preferred_element_type=jnp.float32
    ).astype(jnp.bfloat16)
    outgoing = outgoing.reshape(table_count, slot_count, width)
    if table_count == 2:
        first = lax.axis_index("table") == 0
        own = jnp.where(first, outgoing[0], outgoing[1])
        asked = jnp.where(first, outgoing[1], outgoing[0])
        came = lax.ppermute(asked, "table", [(0, 1), (1, 0)])
        fetched = jnp.concatenate([jnp.where(first, own, came), jnp.where(first, came, own)])
    else:
        fetched = lax.all_to_all(outgoing, "table", split_axis=0, concat_axis=0, tiled=True).reshape(
            fetched_count, width
        )
    dense, slot_grad = local_terms(
        fetched, item_slot, action_id, lengths[0], action_table, w_in, w_proj, w_out, cotangent
    )
    factor = (lax.axis_size("dp") * table_count * lax.axis_size("rep")) ** (-0.5)
    grad_in = dense[0] * factor
    grad_proj = dense[1] * factor
    grad_out = dense[2] * factor
    action_grad = dense[3] * factor
    dp_count = lax.axis_size("dp")
    dp_bits = dp_count.bit_length() - 1
    rows = (grad_in.shape[0] + grad_proj.shape[0] + grad_out.shape[0]) // 2
    pairs = table_count == 2 and lax.axis_size("rep") == 2 and dp_count == 1 << dp_bits
    pairs = pairs and dp_bits > 1
    if pairs and rows % (16 << (dp_bits + 1)) == 0:
        actions = action_grad.shape[0]
        proj_total, in_total, out_total, action_total, returned = combine(
            grad_proj.astype(jnp.bfloat16),
            grad_in.astype(jnp.bfloat16),
            grad_out.astype(jnp.bfloat16),
            action_grad.reshape(actions, 2, width // 2).swapaxes(0, 1),
            slot_grad.reshape(table_count, slot_count, width),
            dp_bits,
        )
        totals = (
            in_total.astype(jnp.float32),
            proj_total.astype(jnp.float32),
            out_total.astype(jnp.float32),
            action_total,
        )
    else:
        returned = lax.all_to_all(
            slot_grad.reshape(table_count, slot_count, width),
            "table",
            split_axis=0,
            concat_axis=0,
            tiled=True,
        )
        shares = (
            lax.psum_scatter(grad_in, "table", scatter_dimension=0, tiled=True),
            lax.psum_scatter(grad_proj, "table", scatter_dimension=0, tiled=True),
            lax.psum_scatter(grad_out, "table", scatter_dimension=0, tiled=True),
            lax.psum_scatter(action_grad, "table", scatter_dimension=1, tiled=True),
        )
        totals = lax.psum((shares[0], shares[1], shares[2], shares[3]), ("dp", "rep"))
    item_grad = jnp.dot(
        fetch_hot.astype(jnp.float32).T,
        returned.reshape(fetched_count, width),
        precision=lax.Precision.HIGH,
    )
    return (item_grad, totals[0], totals[1], totals[2], totals[3])


def solution(mesh):
    return jax.shard_map(
        shards,
        mesh=mesh,
        in_specs=(
            P("table", None),
            P(("dp", "table", "rep"), None),
            P(("dp", "table", "rep"), None),
            P(("dp", "table", "rep")),
            P(("dp", "table", "rep")),
            P(("dp", "table", "rep"), None),
            P(),
            P(),
            P(),
            P(),
            P(("dp", "table", "rep"), None),
        ),
        out_specs=(
            P(("dp", "table", "rep"), None),
            P("table", None),
            P("table", None),
            P("table", None),
            P(None, "table"),
        ),
        check_vma=False,
    )
```
